32 devices in a mesh: grp: 4 (over y, core), wide: 8 (over z, x).
Axes of the slice: x: 2, y: 2, z: 4, core: 2. Of those that a mesh axis runs over, the one named last changes fastest.
Arguments:
- coefficients: bfloat16 [512, 2, 128, 512], P(('grp', 'wide')), may hold values from -6 to 6
- source_blocks: bfloat16 [2, 512, 2, 128, 256], P(None, ('grp', 'wide')), may hold values from -0.25 to 0.25
- target_blocks: bfloat16 [3, 512, 2, 128, 256], P(None, ('grp', 'wide')), may hold values from -0.25 to 0.25
- pair_tables: int32 [2, 32, 16], P(None, ('grp', 'wide')), may hold values from 0 to 15, each once within a row
Outputs:
- target_coeffs: bfloat16 [512, 2, 128, 512], P(('grp', 'wide'))
The draws below stay inside these ranges and needn't reach their ends.
Inputs may be any that keep to these rules, and one draw needn't show every extreme that they name: Each row pair_tables[s, d] is a permutation of the numbers 0 to 15.
All inputs are finite; a program needn't handle non-finite values.
Results may differ from the reference program's by a relative error of at most 0.007.
Values may be sent and summed in bfloat16 or wider, within the bound.
A program may use at most 128 MiB of HBM per device.

```python
import jax
import jax.numpy as jnp
import numpy as np
from jax import lax

R = 128
E = 512
BOX_DEV = 16
SRC_LEVELS = 2
TGT_LEVELS = 3
P_SIZE = 512
N_GRP = 4
N_WIDE = 8
DEVICES = 32


def shard_levels(own_key, dims, cuts, low, largest):
    factor_of = 1.0
    for dim, blocks in cuts:
        draws = jax.random.uniform(jax.random.fold_in(jax.random.fold_in(own_key, 6), dim), (blocks,), jnp.float32, low / len(cuts), largest / len(cuts))
        factor_of = factor_of * jnp.repeat(jnp.exp(draws), dims[dim] // blocks).reshape((-1,) + (1,) * (len(dims) - 1 - dim))
    return factor_of


def scatter_about(key, dims, deviation, reach, shards=(), kind=jnp.bfloat16):
    values = jax.random.normal(key, dims, jnp.float32) * deviation
    if len(shards) > 0:
        values = shard_levels(key, dims, shards, -0.22, 0.18) * values
    return jnp.clip(values, min=-reach, max=reach).astype(kind)


def setup_inputs(seed: int = 0) -> dict:
    seeds = jax.random.split(jax.random.key(seed), 5)
    coefficients = scatter_about(seeds[0], (P_SIZE, 2, R, E), 1.0, 6.0, ((0, 32),))
    source_blocks = scatter_about(seeds[1], (SRC_LEVELS, P_SIZE, 2, R, 2 * R), (4 * R) ** -0.5, 0.25, ((1, 32),))
    target_blocks = scatter_about(seeds[2], (TGT_LEVELS, P_SIZE, 2, R, 2 * R), (4 * R) ** -0.5, 0.25, ((1, 32),))
    pair_tables = jax.vmap(lambda own: jax.random.permutation(own, BOX_DEV))(jax.random.split(seeds[3], SRC_LEVELS * DEVICES)).reshape((SRC_LEVELS, DEVICES, BOX_DEV)).astype(jnp.int32)
    return dict(coefficients=coefficients, source_blocks=source_blocks, target_blocks=target_blocks, pair_tables=pair_tables)


def complex_apply(blocks, stacked):
    matrix = blocks.astype(jnp.float32)
    vector = stacked.astype(jnp.float32)
    real_part = jnp.einsum('nij,njk->nik', matrix[:, 0], vector[:, 0]) - jnp.einsum('nij,njk->nik', matrix[:, 1], vector[:, 1])
    imag_part = jnp.einsum('nij,njk->nik', matrix[:, 0], vector[:, 1]) + jnp.einsum('nij,njk->nik', matrix[:, 1], vector[:, 0])
    return jnp.stack([real_part, imag_part], axis=1).astype(jnp.bfloat16)


def source_block(operands):
    local_boxes, local_blocks, order_row = operands
    picked = jnp.take(local_boxes, order_row.astype(jnp.int32), axis=0)
    count = picked.shape[0]
    paired = picked.reshape((count // 2, 2) + picked.shape[1:])
    joined = jnp.concatenate([paired[:, 0], paired[:, 1]], axis=2)
    joined = jnp.repeat(joined, 2, axis=0)
    return complex_apply(local_blocks, joined)


def reference(coefficients, source_blocks, target_blocks, pair_tables):
    shape_box = coefficients.shape[1:]
    shape_blk = source_blocks.shape[2:]
    current = coefficients.reshape((DEVICES, BOX_DEV) + shape_box)
    for layer_idx in range(SRC_LEVELS):
        blocks_dev = source_blocks[layer_idx].reshape((DEVICES, BOX_DEV) + shape_blk)
        current = lax.map(source_block, (current, blocks_dev, pair_tables[layer_idx]))
    current = current.reshape((N_GRP, N_WIDE, N_WIDE, BOX_DEV // N_WIDE) + shape_box)
    current = current.transpose(0, 2, 1, 3, 4, 5, 6)
    current = current.reshape((N_GRP, N_WIDE * BOX_DEV) + shape_box)
    bit_count = N_GRP.bit_length() - 1
    groups_all = np.arange(N_GRP)
    for layer_idx in range(TGT_LEVELS):
        mask_bit = 1 << (layer_idx % bit_count)
        lower_ids = jnp.asarray(groups_all & ~mask_bit, dtype=jnp.int32)
        upper_ids = jnp.asarray(groups_all | mask_bit, dtype=jnp.int32)
        blocks_grp = target_blocks[layer_idx].reshape((N_GRP, N_WIDE * BOX_DEV) + shape_blk)
        previous = current

        def target_group(operands):
            lower_id, upper_id, group_blocks = operands
            lower_part = lax.dynamic_index_in_dim(previous, lower_id, 0, keepdims=False)
            upper_part = lax.dynamic_index_in_dim(previous, upper_id, 0, keepdims=False)
            joined = jnp.concatenate([lower_part, upper_part], axis=2)
            return complex_apply(group_blocks, joined)

        current = lax.map(target_group, (lower_ids, upper_ids, blocks_grp))
    return current.reshape((N_GRP * N_WIDE * BOX_DEV,) + shape_box)
```

```python
import functools

import jax
import jax.numpy as jnp
from jax import lax
from jax.experimental import pallas as pl
from jax.experimental.pallas import tpu as pltpu
from jax.sharding import PartitionSpec as P

MESH = pl.DeviceIdType.MESH
LOOK_CHUNKS = 2


def flipped(index, other, size):
    total, bit = 0, 1
    while bit < size:
        total = total + ((index // bit) % 2 + (other // bit) % 2) % 2 * bit
        bit *= 2
    return total


def product(matrix, upper_r, lower_r, upper_i, lower_i):
    cols = upper_r.shape[-1]
    right = jnp.concatenate(
        [jnp.concatenate([upper_r, lower_r], axis=0), jnp.concatenate([upper_i, lower_i], axis=0)],
        axis=1,
    )
    both = jnp.dot(matrix, right, preferred_element_type=jnp.float32)
    rank = upper_r.shape[0]
    pairs = []
    for base in range(0, both.shape[0], 2 * rank):
        top, low = both[base : base + rank], both[base + rank : base + 2 * rank]
        real = top[:, :cols] - low[:, cols:]
        imag = top[:, cols:] + low[:, :cols]
        pairs.append((real.astype(jnp.bfloat16), imag.astype(jnp.bfloat16)))
    return pairs


def kernel(
    n_grp, n_wide, tables, coef, sb, tb, out,
    x1, x2, v, a_send, a_recv, l_send, l_recv,
):
    boxes, _, rank, width = coef.shape
    src_levels, tgt_levels = sb.shape[0], tb.shape[0]
    chunks, cols = x1.shape[0], x1.shape[-1]
    per = boxes // n_wide
    units = chunks * n_wide
    bits = n_grp.bit_length() - 1
    g = lax.axis_index("grp")
    w = lax.axis_index("wide")
    mask = [2 ** (t % bits) for t in range(tgt_levels)]
    side = [(g // b) % 2 for b in mask]
    partner = [g + b * (1 - 2 * s) for b, s in zip(mask, side)]

    barrier = pltpu.get_barrier_semaphore()
    for d in range(1, n_wide):
        pl.semaphore_signal(
            barrier, inc=1, device_id=(g, flipped(w, d, n_wide)), device_id_type=MESH
        )
    for t in range(min(tgt_levels, bits)):
        pl.semaphore_signal(barrier, inc=1, device_id=(partner[t], w), device_id_type=MESH)
    pl.semaphore_wait(barrier, n_wide - 1 + min(tgt_levels, bits))

    def source(c):
        for s in range(src_levels):
            def step(m, carry, s=s):
                qa, qb = tables[s, 0, 2 * m], tables[s, 0, 2 * m + 1]
                if s == 0:
                    at = pl.ds(pl.multiple_of(c * cols, cols), cols)
                    parts = [coef[q, h, :, at] for h in range(2) for q in (qa, qb)]
                else:
                    prev = x1 if s % 2 == 1 else x2
                    parts = [prev[c, q, h] for h in range(2) for q in (qa, qb)]
                dest = x1 if s % 2 == 0 else x2
                matrix = sb[s, pl.ds(2 * m, 2)].reshape(4 * rank, 2 * rank)
                for i, (real, imag) in enumerate(product(matrix, *parts)):
                    dest[c, 2 * m + i, 0] = real
                    dest[c, 2 * m + i, 1] = imag
                return carry

            lax.fori_loop(0, boxes // 2, step, 0)
        last = x1 if src_levels % 2 == 1 else x2
        v[0, c * n_wide, side[0]] = last[c, pl.ds(w * per, per)]

    def across(u):
        c, d = u // n_wide, u % n_wide
        peer = flipped(w, d, n_wide)
        last = x1 if src_levels % 2 == 1 else x2
        return pltpu.make_async_remote_copy(
            src_ref=last.at[c, pl.ds(peer * per, per)],
            dst_ref=v.at[0, u, side[0]],
            send_sem=a_send.at[u],
            recv_sem=a_recv.at[u],
            device_id=(g, peer),
            device_id_type=MESH,
        )

    def exchange(t, u):
        return pltpu.make_async_remote_copy(
            src_ref=v.at[t, u, side[t]],
            dst_ref=v.at[t, u, side[t]],
            send_sem=l_send.at[t, u],
            recv_sem=l_recv.at[t, u],
            device_id=(partner[t], w),
            device_id_type=MESH,
        )

    def send_chunk(c):
        def step(d, carry):
            across(c * n_wide + d).start()
            return carry

        lax.fori_loop(1, n_wide, step, 0)

    look = min(LOOK_CHUNKS, chunks)

    def lead(c, carry):
        source(c)

        @pl.when(c < look)
        def _():
            send_chunk(c)

        return carry

    lax.fori_loop(0, chunks, lead, 0)

    def arrive(u):
        @pl.when(u % n_wide > 0)
        def _():
            across(u).wait_recv()

        later = u + look * n_wide

        @pl.when((u % n_wide > 0) & (later < units))
        def _():
            across(later).start()

        exchange(0, u).start()

    def target(t, u):
        exchange(t, u).wait_recv()
        c, d = u // n_wide, u % n_wide
        base = flipped(w, d, n_wide) * per
        for m in range(per):
            matrix = tb[t, base + m].reshape(2 * rank, 2 * rank)
            parts = [v[t, u, half, m, h] for h in range(2) for half in range(2)]
            [(real, imag)] = product(matrix, *parts)
            if t + 1 < tgt_levels:
                v[t + 1, u, side[t + 1], m, 0] = real
                v[t + 1, u, side[t + 1], m, 1] = imag
            else:
                at = pl.ds(pl.multiple_of(c * cols, cols), cols)
                out[base + m, 0, :, at] = real
                out[base + m, 1, :, at] = imag
        if t + 1 < tgt_levels:
            exchange(t + 1, u).start()

    lags, lag = [], 0
    for t in range(tgt_levels):
        lag += 1 if mask[t] == 1 else 2
        lags.append(lag)

    def main(s, carry):
        @pl.when(s < units)
        def _():
            arrive(s)

        for t in range(tgt_levels):
            @pl.when((s >= lags[t]) & (s < units + lags[t]))
            def _(t=t):
                target(t, s - lags[t])

        return carry

    lax.fori_loop(0, units + lags[-1], main, 0)

    def drain(u, carry):
        @pl.when(u % n_wide > 0)
        def _():
            across(u).wait_send()

        for t in range(tgt_levels):
            exchange(t, u).wait_send()
        return carry

    lax.fori_loop(0, units, drain, 0)


def solution(mesh):
    n_grp, n_wide = mesh.shape["grp"], mesh.shape["wide"]

    def on_device(coefficients, source_blocks, target_blocks, pair_tables):
        boxes, _, rank, width = coefficients.shape
        tgt_levels = target_blocks.shape[0]
        cols = min(128, width)
        chunks = width // cols
        units = chunks * n_wide
        levels = source_blocks.shape[0] + tgt_levels
        in_vmem = pl.BlockSpec(memory_space=pltpu.VMEM)
        return pl.pallas_call(
            functools.partial(kernel, n_grp, n_wide),
            out_shape=jax.ShapeDtypeStruct(coefficients.shape, jnp.bfloat16),
            in_specs=[pl.BlockSpec(memory_space=pltpu.SMEM)] + [in_vmem] * 3,
            out_specs=in_vmem,
            scratch_shapes=[
                pltpu.VMEM((chunks, boxes, 2, rank, cols), jnp.bfloat16),
                pltpu.VMEM((chunks, boxes, 2, rank, cols), jnp.bfloat16),
                pltpu.VMEM((tgt_levels, units, 2, boxes // n_wide, 2, rank, cols), jnp.bfloat16),
                pltpu.SemaphoreType.DMA((units,)),
                pltpu.SemaphoreType.DMA((units,)),
                pltpu.SemaphoreType.DMA((tgt_levels, units)),
                pltpu.SemaphoreType.DMA((tgt_levels, units)),
            ],
            compiler_params=pltpu.CompilerParams(
                collective_id=0, has_side_effects=True, vmem_limit_bytes=58 * 2**20
            ),
            cost_estimate=pl.CostEstimate(
                flops=levels * boxes * 16 * rank * rank * width,
                bytes_accessed=2 * (2 * coefficients.size + source_blocks.size + target_blocks.size),
                transcendentals=0,
            ),
        )(pair_tables, coefficients, source_blocks, target_blocks)

    in_specs = (
        P(("grp", "wide"), None, None, None),
        P(None, ("grp", "wide"), None, None, None),
        P(None, ("grp", "wide"), None, None, None),
        P(None, ("grp", "wide"), None),
    )
    out_specs = P(("grp", "wide"), None, None, None)
    return jax.shard_map(
        on_device, mesh=mesh, in_specs=in_specs, out_specs=out_specs, check_vma=False
    )
```

```python
import functools

import jax
import jax.numpy as jnp
from jax import lax
from jax.experimental import pallas as pl
from jax.experimental.pallas import tpu as pltpu
from jax.sharding import PartitionSpec as P

MESH = pl.DeviceIdType.MESH
LOOK_CHUNKS = 1


def flipped(index, other, size):
    total, bit = 0, 1
    while bit < size:
        total = total + ((index // bit) % 2 + (other // bit) % 2) % 2 * bit
        bit *= 2
    return total


def product(matrix, upper_r, lower_r, upper_i, lower_i):
    cols = upper_r.shape[-1]
    right = jnp.concatenate(
        [jnp.concatenate([upper_r, lower_r], axis=0), jnp.concatenate([upper_i, lower_i], axis=0)],
        axis=1,
    )
    both = jnp.dot(matrix, right, preferred_element_type=jnp.float32)
    rank = upper_r.shape[0]
    pairs = []
    for base in range(0, both.shape[0], 2 * rank):
        top, low = both[base : base + rank], both[base + rank : base + 2 * rank]
        real = top[:, :cols] - low[:, cols:]
        imag = top[:, cols:] + low[:, :cols]
        pairs.append((real.astype(jnp.bfloat16), imag.astype(jnp.bfloat16)))
    return pairs


def kernel(
    n_grp, n_wide, tables, coef, sb, tb, out,
    x1, x2, v, a_send, a_recv, l_send, l_recv,
):
    boxes, _, rank, width = coef.shape
    src_levels, tgt_levels = sb.shape[0], tb.shape[0]
    chunks, cols = x1.shape[0], x1.shape[-1]
    per = boxes // n_wide
    units = chunks * n_wide
    bits = n_grp.bit_length() - 1
    g = lax.axis_index("grp")
    w = lax.axis_index("wide")
    mask = [2 ** (t % bits) for t in range(tgt_levels)]
    side = [(g // b) % 2 for b in mask]
    partner = [g + b * (1 - 2 * s) for b, s in zip(mask, side)]

    barrier = pltpu.get_barrier_semaphore()
    for d in range(1, n_wide):
        pl.semaphore_signal(
            barrier, inc=1, device_id=(g, flipped(w, d, n_wide)), device_id_type=MESH
        )
    for t in range(min(tgt_levels, bits)):
        pl.semaphore_signal(barrier, inc=1, device_id=(partner[t], w), device_id_type=MESH)
    pl.semaphore_wait(barrier, n_wide - 1 + min(tgt_levels, bits))

    def source(c):
        for s in range(src_levels):
            def step(m, carry, s=s):
                qa, qb = tables[s, 0, 2 * m], tables[s, 0, 2 * m + 1]
                if s == 0:
                    at = pl.ds(pl.multiple_of(c * cols, cols), cols)
                    parts = [coef[q, h, :, at] for h in range(2) for q in (qa, qb)]
                else:
                    prev = x1 if s % 2 == 1 else x2
                    parts = [prev[c, q, h] for h in range(2) for q in (qa, qb)]
                dest = x1 if s % 2 == 0 else x2
                matrix = sb[s, pl.ds(2 * m, 2)].reshape(4 * rank, 2 * rank)
                for i, (real, imag) in enumerate(product(matrix, *parts)):
                    dest[c, 2 * m + i, 0] = real
                    dest[c, 2 * m + i, 1] = imag
                return carry

            lax.fori_loop(0, boxes // 2, step, 0)
        last = x1 if src_levels % 2 == 1 else x2
        v[0, c * n_wide, side[0]] = last[c, pl.ds(w * per, per)]

    def across(u):
        c, d = u // n_wide, u % n_wide
        peer = flipped(w, d, n_wide)
        last = x1 if src_levels % 2 == 1 else x2
        return pltpu.make_async_remote_copy(
            src_ref=last.at[c, pl.ds(peer * per, per)],
            dst_ref=v.at[0, u, side[0]],
            send_sem=a_send.at[u],
            recv_sem=a_recv.at[u],
            device_id=(g, peer),
            device_id_type=MESH,
        )

    def exchange(t, u):
        return pltpu.make_async_remote_copy(
            src_ref=v.at[t, u, side[t]],
            dst_ref=v.at[t, u, side[t]],
            send_sem=l_send.at[t, u],
            recv_sem=l_recv.at[t, u],
            device_id=(partner[t], w),
            device_id_type=MESH,
        )

    def send_chunk(c):
        def step(d, carry):
            across(c * n_wide + d).start()
            return carry

        lax.fori_loop(1, n_wide, step, 0)

    look = min(LOOK_CHUNKS, chunks)

    def lead(c, carry):
        source(c)

        @pl.when(c < look)
        def _():
            send_chunk(c)

        return carry

    lax.fori_loop(0, chunks, lead, 0)

    def arrive(u):
        @pl.when(u % n_wide > 0)
        def _():
            across(u).wait_recv()

        later = u + look * n_wide

        @pl.when((u % n_wide > 0) & (later < units))
        def _():
            across(later).start()

        exchange(0, u).start()

    def target(t, u):
        exchange(t, u).wait_recv()
        c, d = u // n_wide, u % n_wide
        base = flipped(w, d, n_wide) * per
        for m in range(per):
            matrix = tb[t, base + m].reshape(2 * rank, 2 * rank)
            parts = [v[t, u, half, m, h] for h in range(2) for half in range(2)]
            [(real, imag)] = product(matrix, *parts)
            if t + 1 < tgt_levels:
                v[t + 1, u, side[t + 1], m, 0] = real
                v[t + 1, u, side[t + 1], m, 1] = imag
            else:
                at = pl.ds(pl.multiple_of(c * cols, cols), cols)
                out[base + m, 0, :, at] = real
                out[base + m, 1, :, at] = imag
        if t + 1 < tgt_levels:
            exchange(t + 1, u).start()

    lags, lag = [], 0
    for t in range(tgt_levels):
        lag += 1 if mask[t] == 1 else 2
        lags.append(lag)

    def main(s, carry):
        @pl.when(s < units)
        def _():
            arrive(s)

        for t in range(tgt_levels):
            @pl.when((s >= lags[t]) & (s < units + lags[t]))
            def _(t=t):
                target(t, s - lags[t])

        return carry

    lax.fori_loop(0, units + lags[-1], main, 0)

    def drain(u, carry):
        @pl.when(u % n_wide > 0)
        def _():
            across(u).wait_send()

        for t in range(tgt_levels):
            exchange(t, u).wait_send()
        return carry

    lax.fori_loop(0, units, drain, 0)


def solution(mesh):
    n_grp, n_wide = mesh.shape["grp"], mesh.shape["wide"]

    def on_device(coefficients, source_blocks, target_blocks, pair_tables):
        boxes, _, rank, width = coefficients.shape
        tgt_levels = target_blocks.shape[0]
        cols = min(128, width)
        chunks = width // cols
        units = chunks * n_wide
        levels = source_blocks.shape[0] + tgt_levels
        in_vmem = pl.BlockSpec(memory_space=pltpu.VMEM)
        return pl.pallas_call(
            functools.partial(kernel, n_grp, n_wide),
            out_shape=jax.ShapeDtypeStruct(coefficients.shape, jnp.bfloat16),
            in_specs=[pl.BlockSpec(memory_space=pltpu.SMEM)] + [in_vmem] * 3,
            out_specs=in_vmem,
            scratch_shapes=[
                pltpu.VMEM((chunks, boxes, 2, rank, cols), jnp.bfloat16),
                pltpu.VMEM((chunks, boxes, 2, rank, cols), jnp.bfloat16),
                pltpu.VMEM((tgt_levels, units, 2, boxes // n_wide, 2, rank, cols), jnp.bfloat16),
                pltpu.SemaphoreType.DMA((units,)),
                pltpu.SemaphoreType.DMA((units,)),
                pltpu.SemaphoreType.DMA((tgt_levels, units)),
                pltpu.SemaphoreType.DMA((tgt_levels, units)),
            ],
            compiler_params=pltpu.CompilerParams(
                collective_id=0, has_side_effects=True, vmem_limit_bytes=58 * 2**20
            ),
            cost_estimate=pl.CostEstimate(
                flops=levels * boxes * 16 * rank * rank * width,
                bytes_accessed=2 * (2 * coefficients.size + source_blocks.size + target_blocks.size),
                transcendentals=0,
            ),
        )(pair_tables, coefficients, source_blocks, target_blocks)

    in_specs = (
        P(("grp", "wide"), None, None, None),
        P(None, ("grp", "wide"), None, None, None),
        P(None, ("grp", "wide"), None, None, None),
        P(None, ("grp", "wide"), None),
    )
    out_specs = P(("grp", "wide"), None, None, None)
    return jax.shard_map(
        on_device, mesh=mesh, in_specs=in_specs, out_specs=out_specs, check_vma=False
    )
```

```python
import functools

import jax
import jax.numpy as jnp
from jax import lax
from jax.experimental import pallas as pl
from jax.experimental.pallas import tpu as pltpu
from jax.sharding import PartitionSpec as P

MESH = pl.DeviceIdType.MESH
LOOK = 6
HOLD = 4
NEAR = 2


def flipped(index, other, size):
    total, bit = 0, 1
    while bit < size:
        total = total + ((index // bit) % 2 + (other // bit) % 2) % 2 * bit
        bit *= 2
    return total


def product(matrix, upper_r, lower_r, upper_i, lower_i):
    cols = upper_r.shape[-1]
    right = jnp.concatenate(
        [jnp.concatenate([upper_r, lower_r], axis=0), jnp.concatenate([upper_i, lower_i], axis=0)],
        axis=1,
    )
    both = jnp.dot(matrix, right, preferred_element_type=jnp.float32)
    rank = upper_r.shape[0]
    pairs = []
    for base in range(0, both.shape[0], 2 * rank):
        top, low = both[base : base + rank], both[base + rank : base + 2 * rank]
        real = top[:, :cols] - low[:, cols:]
        imag = top[:, cols:] + low[:, :cols]
        pairs.append((real.astype(jnp.bfloat16), imag.astype(jnp.bfloat16)))
    return pairs


def kernel(
    n_grp, n_wide, tables, coef, sb, tb_hbm, out_hbm,
    tb, tb_sem, out, out_sem, x1, x2, v, a_send, a_recv, l_send, l_recv,
):
    boxes, _, rank, width = coef.shape
    src_levels, tgt_levels = sb.shape[0], tb.shape[0]
    chunks, cols = x1.shape[0], x1.shape[-1]
    per = boxes // n_wide
    units = chunks * n_wide
    bits = n_grp.bit_length() - 1
    g = lax.axis_index("grp")
    w = lax.axis_index("wide")
    mask = [2 ** (t % bits) for t in range(tgt_levels)]
    side = [(g // b) % 2 for b in mask]
    partner = [g + b * (1 - 2 * s) for b, s in zip(mask, side)]

    blocks_in = pltpu.make_async_copy(tb_hbm, tb, tb_sem)
    blocks_in.start()

    barrier = pltpu.get_barrier_semaphore()
    for d in range(1, n_wide):
        pl.semaphore_signal(
            barrier, inc=1, device_id=(g, flipped(w, d, n_wide)), device_id_type=MESH
        )
    for t in range(min(tgt_levels, bits)):
        pl.semaphore_signal(barrier, inc=1, device_id=(partner[t], w), device_id_type=MESH)
    pl.semaphore_wait(barrier, n_wide - 1 + min(tgt_levels, bits))

    def source(c):
        for s in range(src_levels):
            def step(m, carry, s=s):
                qa, qb = tables[s, 0, 2 * m], tables[s, 0, 2 * m + 1]
                if s == 0:
                    at = pl.ds(pl.multiple_of(c * cols, cols), cols)
                    parts = [coef[q, h, :, at] for h in range(2) for q in (qa, qb)]
                else:
                    prev = x1 if s % 2 == 1 else x2
                    parts = [prev[c, q, h] for h in range(2) for q in (qa, qb)]
                dest = x1 if s % 2 == 0 else x2
                matrix = sb[s, pl.ds(2 * m, 2)].reshape(4 * rank, 2 * rank)
                for i, (real, imag) in enumerate(product(matrix, *parts)):
                    dest[c, 2 * m + i, 0] = real
                    dest[c, 2 * m + i, 1] = imag
                return carry

            lax.fori_loop(0, boxes // 2, step, 0)
        last = x1 if src_levels % 2 == 1 else x2
        v[0, c * n_wide, side[0]] = last[c, pl.ds(w * per, per)]

    def across(u):
        c, d = u // n_wide, u % n_wide
        peer = flipped(w, d, n_wide)
        last = x1 if src_levels % 2 == 1 else x2
        return pltpu.make_async_remote_copy(
            src_ref=last.at[c, pl.ds(peer * per, per)],
            dst_ref=v.at[0, u, side[0]],
            send_sem=a_send.at[u],
            recv_sem=a_recv.at[u],
            device_id=(g, peer),
            device_id_type=MESH,
        )

    def result(u):
        c, d = u // n_wide, u % n_wide
        base = flipped(w, d, n_wide) * per
        at = pl.ds(pl.multiple_of(c * cols, cols), cols)
        return pltpu.make_async_copy(
            out.at[u], out_hbm.at[pl.ds(base, per), :, :, at], out_sem.at[u]
        )

    def exchange(t, u):
        return pltpu.make_async_remote_copy(
            src_ref=v.at[t, u, side[t]],
            dst_ref=v.at[t, u, side[t]],
            send_sem=l_send.at[t, u],
            recv_sem=l_recv.at[t, u],
            device_id=(partner[t], w),
            device_id_type=MESH,
        )

    far = n_wide - NEAR
    n_near, n_far = chunks * NEAR, chunks * far
    look = min(LOOK, far)

    def far_unit(f):
        return f // far * n_wide + NEAR + f % far

    def unit(s):
        late = (s - n_near + units) // units
        near_u = s // NEAR * n_wide + s % NEAR
        return (1 - late) * near_u + late * far_unit(s - late * n_near)

    def send_near(c):
        for d in range(1, NEAR):
            across(c * n_wide + d).start()

    def arrive(s):
        u = unit(s)

        @pl.when((s % NEAR == 0) & (s // NEAR + 1 < chunks))
        def _():
            source(s // NEAR + 1)
            send_near(s // NEAR + 1)

        @pl.when(u % n_wide > 0)
        def _():
            across(u).wait_recv()

        later = s - HOLD + look

        @pl.when((s >= HOLD) & (later < n_far))
        def _():
            across(far_unit(later)).start()

        exchange(0, u).start()

    def first(f, carry):
        across(far_unit(f)).start()
        return carry

    source(0)
    lax.fori_loop(0, look, first, 0)
    send_near(0)
    blocks_in.wait()

    def target(t, u):
        exchange(t, u).wait_recv()
        c, d = u // n_wide, u % n_wide
        base = flipped(w, d, n_wide) * per
        for m in range(per):
            matrix = tb[t, base + m].reshape(2 * rank, 2 * rank)
            parts = [v[t, u, half, m, h] for h in range(2) for half in range(2)]
            [(real, imag)] = product(matrix, *parts)
            if t + 1 < tgt_levels:
                v[t + 1, u, side[t + 1], m, 0] = real
                v[t + 1, u, side[t + 1], m, 1] = imag
            else:
                out[u, m, 0] = real
                out[u, m, 1] = imag
        if t + 1 < tgt_levels:
            exchange(t + 1, u).start()
        else:
            result(u).start()

    lags, lag = [], 0
    for t in range(tgt_levels):
        lag += 1 if mask[t] == 1 else 2
        lags.append(lag)

    def main(s, carry):
        @pl.when(s < units)
        def _():
            arrive(s)

        for t in range(tgt_levels):
            @pl.when((s >= lags[t]) & (s < units + lags[t]))
            def _(t=t):
                target(t, unit(s - lags[t]))

        return carry

    lax.fori_loop(0, units + lags[-1], main, 0)

    def drain(u, carry):
        @pl.when(u % n_wide > 0)
        def _():
            across(u).wait_send()

        for t in range(tgt_levels):
            exchange(t, u).wait_send()
        result(u).wait()
        return carry

    lax.fori_loop(0, units, drain, 0)


def solution(mesh):
    n_grp, n_wide = mesh.shape["grp"], mesh.shape["wide"]

    def on_device(coefficients, source_blocks, target_blocks, pair_tables):
        boxes, _, rank, width = coefficients.shape
        tgt_levels = target_blocks.shape[0]
        cols = min(128, width)
        chunks = width // cols
        units = chunks * n_wide
        levels = source_blocks.shape[0] + tgt_levels
        in_vmem = pl.BlockSpec(memory_space=pltpu.VMEM)
        return pl.pallas_call(
            functools.partial(kernel, n_grp, n_wide),
            out_shape=jax.ShapeDtypeStruct(coefficients.shape, jnp.bfloat16),
            in_specs=[pl.BlockSpec(memory_space=pltpu.SMEM)] + [in_vmem] * 2 + [pl.BlockSpec(memory_space=pl.ANY)],
            out_specs=pl.BlockSpec(memory_space=pl.ANY),
            scratch_shapes=[
                pltpu.VMEM(target_blocks.shape, jnp.bfloat16),
                pltpu.SemaphoreType.DMA,
                pltpu.VMEM((units, boxes // n_wide, 2, rank, cols), jnp.bfloat16),
                pltpu.SemaphoreType.DMA((units,)),
                pltpu.VMEM((chunks, boxes, 2, rank, cols), jnp.bfloat16),
                pltpu.VMEM((chunks, boxes, 2, rank, cols), jnp.bfloat16),
                pltpu.VMEM((tgt_levels, units, 2, boxes // n_wide, 2, rank, cols), jnp.bfloat16),
                pltpu.SemaphoreType.DMA((units,)),
                pltpu.SemaphoreType.DMA((units,)),
                pltpu.SemaphoreType.DMA((tgt_levels, units)),
                pltpu.SemaphoreType.DMA((tgt_levels, units)),
            ],
            compiler_params=pltpu.CompilerParams(
                collective_id=0, has_side_effects=True, vmem_limit_bytes=58 * 2**20
            ),
            cost_estimate=pl.CostEstimate(
                flops=levels * boxes * 16 * rank * rank * width,
                bytes_accessed=2 * (2 * coefficients.size + source_blocks.size + target_blocks.size),
                transcendentals=0,
            ),
        )(pair_tables, coefficients, source_blocks, target_blocks)

    in_specs = (
        P(("grp", "wide"), None, None, None),
        P(None, ("grp", "wide"), None, None, None),
        P(None, ("grp", "wide"), None, None, None),
        P(None, ("grp", "wide"), None),
    )
    out_specs = P(("grp", "wide"), None, None, None)
    return jax.shard_map(
        on_device, mesh=mesh, in_specs=in_specs, out_specs=out_specs, check_vma=False
    )
```
